128 devices in a mesh: worker: 4 (over z_lo, core), tp: 32 (over z_hi, y, x).
Axes of the slice: x: 4, y: 4, z: 4 (z_hi: 2, z_lo: 2; z = z_hi * 2 + z_lo), core: 2. Of those that a mesh axis runs over, the one named last changes fastest.
Arguments:
- global_params: float32 [512, 4608], P('tp'), may hold values from -6 to 6
- momentum: float32 [512, 4608], P('tp'), may hold values from -3 to 3
- local_params: float32 [4, 512, 4608], P('worker', 'tp'), may hold values from -6 to 6
- inputs: bfloat16 [4, 1024, 4608], P('worker', 'tp'), may hold values from -6 to 6
- out_grad: bfloat16 [4, 1024, 4608], P('worker', 'tp'), may hold values from -6 to 6
- token_ids: int32 [4, 1024], P('worker', 'tp'), may hold values from 0 to 255999, as said below
- gain: float32 [4, 4608], P('worker'), may hold values from 0.1 to 1.9
- w_gate: bfloat16 [4, 9216, 4608], P('worker', 'tp'), may hold values from -0.09375 to 0.09375
- w_up: bfloat16 [4, 9216, 4608], P('worker', 'tp'), may hold values from -0.09375 to 0.09375
- w_down: bfloat16 [4, 9216, 4608], P('worker', 'tp'), may hold values from -0.0625 to 0.0625
Outputs:
- new_params: float32 [512, 4608], P('tp')
- new_momentum: float32 [512, 4608], P('tp')
- ffn_out: bfloat16 [4, 1024, 4608], P('worker', 'tp')
- grad_input: bfloat16 [4, 1024, 4608], P('worker', 'tp')
- grad_gain: float32 [4, 4608], P('worker')
- grad_gate: bfloat16 [4, 9216, 4608], P('worker', 'tp')
- grad_up: bfloat16 [4, 9216, 4608], P('worker', 'tp')
- grad_down: bfloat16 [4, 9216, 4608], P('worker', 'tp')
The draws below stay inside these ranges and needn't reach their ends.
Inputs may be any that keep to these rules, and one draw needn't show every extreme that they name: `token_ids`: each worker's row of 1024 ids ends in a run of padding ids 0 that is 128 to 512 positions long; every other id lies in 1 to 255999.
All inputs are finite; a program needn't handle non-finite values.
Results may differ from the reference program's by a relative error of at most 0.025.
Values may be sent and summed in bfloat16 or wider, within the bound.
No kernel may reach another device: no remote copies, remote signals or barrier semaphores. Data moves between devices by JAX's collectives and lax.ppermute only.
A program may use at most 192 MiB of HBM per device.

```python
import jax
import jax.numpy as jnp
from jax import lax

D = 4608
VOCAB = 256000
SLAB = 9216
TOK = 1024
ROWS = 512
N_WORKER = 4
N_TP = 32


def draw_token_ids(key, part):
    key = jax.random.fold_in(key, 7)
    id_key, tail_key, spot_key = jax.random.split(key, 3)
    raw_ids = jax.random.randint(id_key, (N_WORKER, TOK), 1, VOCAB)
    tails = jax.random.randint(tail_key, (N_WORKER, 1), TOK // 8, TOK // 2 + 1)
    spots = jax.random.randint(spot_key, (N_WORKER, 1), 0, TOK - TOK // 2)
    position = jnp.arange(TOK)[None, :]
    with_top = jnp.where(position == spots, VOCAB - 1, raw_ids)
    return jnp.where(position >= TOK - tails, 0, with_top).astype(jnp.int32)


def steps_of(stream_key, dims, cuts, low, top_value):
    def one(dim, blocks):
        draws = jax.random.uniform(jax.random.fold_in(jax.random.fold_in(stream_key, 6), dim), (blocks,), jnp.float32, low / len(cuts), top_value / len(cuts))
        return jnp.repeat(jnp.exp(draws), dims[dim] // blocks).reshape((-1,) + (1,) * (len(dims) - dim - 1))

    loudness = one(*cuts[0])
    for cut in cuts[1:]:
        loudness = loudness * one(*cut)
    return loudness


def noise(key, shape, width, bound, cuts=(), dtype=jnp.bfloat16):
    result = jax.random.normal(key, shape, jnp.float32) * width
    if len(cuts) > 0:
        result = steps_of(key, shape, cuts, -0.22, 0.18) * result
    return jnp.clip(result, min=-bound, max=bound).astype(dtype)


def setup_inputs(seed: int = 0) -> dict:
    arg_keys = jax.random.split(jax.random.key(seed), 11)
    global_params = noise(arg_keys[0], (ROWS, D), 1.0, 6.0, ((0, 32),), jnp.float32)
    momentum = noise(arg_keys[1], (ROWS, D), 0.5, 3.0, ((0, 32),), jnp.float32)
    local_params = noise(arg_keys[2], (N_WORKER, ROWS, D), 1.0, 6.0, ((0, 4), (1, 32)), jnp.float32)
    inputs = noise(arg_keys[3], (N_WORKER, TOK, D), 1.0, 6.0, ((0, 4), (1, 32)))
    out_grad = noise(arg_keys[4], (N_WORKER, TOK, D), 1.0, 6.0, ((0, 4), (1, 32)))
    token_ids = draw_token_ids(jax.random.fold_in(arg_keys[10], 71), 0)
    gain = jnp.clip(1.0 + 0.18 * jax.random.normal(arg_keys[6], (N_WORKER, D), jnp.float32), 0.1, 1.9)
    w_gate = noise(arg_keys[7], (N_WORKER, SLAB, D), D ** -0.5, 0.09375, ((0, 4), (1, 32)))
    w_up = noise(arg_keys[8], (N_WORKER, SLAB, D), D ** -0.5, 0.09375, ((0, 4), (1, 32)))
    w_down = noise(arg_keys[9], (N_WORKER, SLAB, D), SLAB ** -0.5, 0.0625, ((0, 4), (1, 32)))
    return {"global_params": global_params, "momentum": momentum, "local_params": local_params, "inputs": inputs, "out_grad": out_grad, "token_ids": token_ids, "gain": gain, "w_gate": w_gate, "w_up": w_up, "w_down": w_down}


OUTER_RATE = 0.7
OUTER_MOMENTUM = 0.9
NORM_EPS = 1e-06

def gelu_tanh(values):
    return jax.nn.gelu(values, approximate=True)

def gelu_grad(pre_act, upstream):
    outputs = jax.vjp(gelu_tanh, pre_act)
    return outputs[1](upstream)[0]

def group_sum(lefts, rights):
    group_width = lefts[0].shape[1] // N_TP
    token_count = lefts[0].shape[0]
    split_left = tuple((member.reshape(token_count, N_TP, group_width).transpose(1, 0, 2) for member in lefts))
    split_right = tuple((member.reshape(N_TP, group_width, member.shape[1]) for member in rights))

    def add_group(running, pieces):
        partial_sum = jnp.zeros((token_count, rights[0].shape[1]), jnp.float32)
        for left_block, right_block in zip(pieces[0], pieces[1]):
            partial_sum = partial_sum + jnp.dot(left_block, right_block, preferred_element_type=jnp.float32)
        rounded = lax.optimization_barrier(partial_sum.astype(jnp.bfloat16))
        return (running + rounded.astype(jnp.float32), None)
    zero_sum = jnp.zeros((token_count, rights[0].shape[1]), jnp.float32)
    running, unused = lax.scan(add_group, zero_sum, (split_left, split_right))
    return running

def inner_step(tokens_in, grad_out, ids_row, gain_row, gate_w, up_w, down_w):
    tokens_f = tokens_in.astype(jnp.float32)
    inv_rms = lax.rsqrt(lax.optimization_barrier(jnp.mean(tokens_f * tokens_f, axis=1, keepdims=True)) + NORM_EPS)
    scaled = tokens_f * inv_rms
    normed = (scaled * gain_row[None, :]).astype(jnp.bfloat16)
    gate_pre = jnp.dot(normed, gate_w.T, preferred_element_type=jnp.float32)
    up_pre = jnp.dot(normed, up_w.T, preferred_element_type=jnp.float32)
    activated = gelu_tanh(gate_pre)
    hidden = (activated * up_pre).astype(jnp.bfloat16)
    ffn_sum = group_sum((hidden,), (down_w,))
    masked = jnp.where((ids_row != 0)[:, None], grad_out, jnp.zeros_like(grad_out))
    hid_grad = jnp.dot(masked, down_w.T, preferred_element_type=jnp.float32)
    grad_down = jnp.dot(hidden.T, masked, preferred_element_type=jnp.float32).astype(jnp.bfloat16)
    gate_grad = gelu_grad(gate_pre, hid_grad * up_pre).astype(jnp.bfloat16)
    up_grad = (hid_grad * activated).astype(jnp.bfloat16)
    grad_gate = jnp.dot(gate_grad.T, normed, preferred_element_type=jnp.float32).astype(jnp.bfloat16)
    grad_up = jnp.dot(up_grad.T, normed, preferred_element_type=jnp.float32).astype(jnp.bfloat16)
    normed_grad = group_sum((gate_grad, up_grad), (gate_w, up_w))
    grad_gain = lax.optimization_barrier(jnp.sum(normed_grad * scaled, axis=0))
    weighted = normed_grad * gain_row[None, :]
    centred = weighted - scaled * lax.optimization_barrier(jnp.mean(weighted * scaled, axis=1, keepdims=True))
    grad_input = (inv_rms * centred).astype(jnp.bfloat16)
    return (ffn_sum.astype(jnp.bfloat16), grad_input, grad_gain, grad_gate, grad_up, grad_down)

def reference(global_params, momentum, local_params, inputs, out_grad, token_ids, gain, w_gate, w_up, w_down):
    average = lax.optimization_barrier(jnp.sum(global_params[None] - local_params, axis=0)) / N_WORKER
    new_momentum = OUTER_MOMENTUM * momentum + average
    new_params = global_params - OUTER_RATE * (average + OUTER_MOMENTUM * new_momentum)
    results = [inner_step(inputs[worker], out_grad[worker], token_ids[worker], gain[worker], w_gate[worker], w_up[worker], w_down[worker]) for worker in range(N_WORKER)]
    stacked = [jnp.stack([entry[place] for entry in results]) for place in range(6)]
    return (new_params, new_momentum, stacked[0], stacked[1], stacked[2], stacked[3], stacked[4], stacked[5])
```

```python
import jax
import jax.numpy as jnp
from jax import lax
from jax.sharding import PartitionSpec as P

OUTER_RATE = 0.7
OUTER_MOMENTUM = 0.9
NORM_EPS = 1e-06

SIDE_Z, SIDE_Y, SIDE_X = 2, 4, 4


def gelu_tanh(values):
    return jax.nn.gelu(values, approximate=True)


def gelu_grad(pre_act, upstream):
    outputs = jax.vjp(gelu_tanh, pre_act)
    return outputs[1](upstream)[0]


def place(z, y, x):
    return (z % SIDE_Z) * SIDE_Y * SIDE_X + (y % SIDE_Y) * SIDE_X + x % SIDE_X


def shift(block, axis, by):
    step = {"z": 0, "y": 0, "x": 0}
    step[axis] = by
    pairs = [
        (place(z, y, x), place(z + step["z"], y + step["y"], x + step["x"]))
        for z in range(SIDE_Z)
        for y in range(SIDE_Y)
        for x in range(SIDE_X)
    ]
    return lax.ppermute(block, "tp", pairs)


def after(value, *others):
    return lax.optimization_barrier((value, others))[0]


def gather_small(block, axis):
    return jnp.concatenate(
        [block, shift(block, axis, 1), shift(block, axis, -1), shift(block, axis, 2)], axis=0
    )


def gather_big(block, axis):
    half = block.shape[0] // 2
    ahead = shift(block, axis, 1)
    behind = shift(block, axis, -1)
    far_low = shift(ahead[:half], axis, 1)
    far_high = shift(behind[half:], axis, -1)
    return [block, ahead, behind, far_low, far_high]


def gather_near(rows, other):
    half = rows.shape[0] // 2
    first = jnp.concatenate([rows[:half], other[:half]], axis=0)
    second = jnp.concatenate([rows[half:], other[half:]], axis=0)
    return lax.optimization_barrier((gather_small(first, "x"), gather_small(second, "y")))


def gather_far(first, second):
    return gather_big(first, "y") + gather_big(second, "x")


def all_sum(row):
    for axis in ("x", "y"):
        row = row + shift(row, axis, 1) + shift(row, axis, -1) + shift(row, axis, 2)
    return row + shift(row, "z", 1)


def total(*terms):
    result = terms[0].astype(jnp.float32)
    for term in terms[1:]:
        result = result + term.astype(jnp.float32)
    return result.astype(terms[0].dtype)


def scatter_big(rows, axis):
    size = rows.shape[0] // 4
    half = size // 2
    own, behind, ahead, far = (rows[i * size : (i + 1) * size] for i in range(4))
    got_up = shift(jnp.concatenate([far[:half], ahead[half:]], axis=0), axis, 1)
    got_down = shift(jnp.concatenate([far[half:], behind[:half]], axis=0), axis, -1)
    last_up = shift(total(ahead[:half], got_up[:half]), axis, 1)
    last_down = shift(total(behind[half:], got_down[:half]), axis, -1)
    low = total(own[:half], last_up, got_down[half:])
    high = total(own[half:], got_up[half:], last_down)
    return jnp.concatenate([low, high], axis=0)


def scatter_small(rows, axis):
    size = rows.shape[0] // 4
    own, behind, ahead, far = (rows[i * size : (i + 1) * size] for i in range(4))
    return total(own, shift(ahead, axis, 1), shift(behind, axis, -1), shift(far, axis, 2))


def scatter(rows):
    half = rows.shape[0] // 2
    first = scatter_small(scatter_big(rows[:half], "y"), "x")
    second = scatter_small(scatter_big(rows[half:], "x"), "y")
    cut = first.shape[0] // 2
    other = shift(jnp.concatenate([first[cut:], second[cut:]], axis=0), "z", 1)
    own = jnp.concatenate([first[:cut], second[:cut]], axis=0)
    return own, other


def dot(left, right, contract, dtype=jnp.float32):
    return lax.dot_general(
        left, right, ((contract[0], contract[1]), ((), ())), preferred_element_type=jnp.float32
    ).astype(dtype)


def local(
    global_params, momentum, local_params, inputs, out_grad, token_ids, gain, w_gate, w_up, w_down
):
    delta = global_params - local_params[0]
    workers = lax.axis_size("worker")
    average = lax.psum(delta.astype(jnp.bfloat16), "worker").astype(jnp.float32) / workers
    new_momentum = OUTER_MOMENTUM * momentum + average
    new_params = global_params - OUTER_RATE * (average + OUTER_MOMENTUM * new_momentum)
    gain_row = gain[0]
    gate_w = w_gate[0]
    up_w = w_up[0]
    down_w = w_down[0]
    tokens_f = inputs[0].astype(jnp.float32)
    inv_rms = lax.rsqrt(jnp.mean(tokens_f * tokens_f, axis=1, keepdims=True) + NORM_EPS)
    scaled = tokens_f * inv_rms
    normed = (scaled * gain_row[None, :]).astype(jnp.bfloat16)
    masked = jnp.where((token_ids[0] != 0)[:, None], out_grad[0], jnp.zeros_like(out_grad[0]))
    last, first = ((1,), (1,)), ((0,), (0,))
    plain = ((1,), (0,))
    normed_other = shift(normed, "z", 1)
    masked_other = shift(after(masked, normed_other), "z", 1)
    pieces = gather_far(*gather_near(normed, normed_other))
    masked, masked_other = after((masked, masked_other), pieces[1], pieces[6])
    normed_all = jnp.concatenate(pieces, axis=0)
    masked_all = jnp.concatenate(gather_far(*gather_near(masked, masked_other)), axis=0)
    gate_pre = dot(normed_all, gate_w, last)
    up_pre = dot(normed_all, up_w, last)
    activated = gelu_tanh(gate_pre)
    hidden = (activated * up_pre).astype(jnp.bfloat16)
    ffn_shares = dot(hidden, down_w, plain, jnp.bfloat16)
    ffn_own, ffn_other = scatter(ffn_shares)
    ffn_sum = total(ffn_own, ffn_other)
    masked_all = after(masked_all, ffn_shares)
    hid_grad = dot(masked_all, down_w, last)
    gate_grad = gelu_grad(gate_pre, hid_grad * up_pre).astype(jnp.bfloat16)
    up_grad = (hid_grad * activated).astype(jnp.bfloat16)
    shares = (dot(gate_grad, gate_w, plain) + dot(up_grad, up_w, plain)).astype(jnp.bfloat16)
    grad_own, grad_other = scatter(shares)
    grad_down = dot(hidden, masked_all, first, jnp.bfloat16)
    grad_gate = dot(gate_grad, normed_all, first, jnp.bfloat16)
    grad_up = dot(up_grad, normed_all, first, jnp.bfloat16)
    gain_share = jnp.sum(
        grad_gate.astype(jnp.float32) * gate_w.astype(jnp.float32)
        + grad_up.astype(jnp.float32) * up_w.astype(jnp.float32),
        axis=0,
    )
    grad_gain = all_sum(gain_share[None])[0] / gain_row
    normed_grad = grad_own.astype(jnp.float32) + grad_other.astype(jnp.float32)
    weighted = normed_grad * gain_row[None, :]
    centred = weighted - scaled * jnp.mean(weighted * scaled, axis=1, keepdims=True)
    grad_input = (inv_rms * centred).astype(jnp.bfloat16)
    return (
        new_params,
        new_momentum,
        ffn_sum[None],
        grad_input[None],
        grad_gain[None],
        grad_gate[None],
        grad_up[None],
        grad_down[None],
    )


def solution(mesh):
    placed = (
        P("tp", None),
        P("tp", None),
        P("worker", "tp", None),
        P("worker", "tp", None),
        P("worker", "tp", None),
        P("worker", "tp"),
        P("worker", None),
        P("worker", "tp", None),
        P("worker", "tp", None),
        P("worker", "tp", None),
    )
    return jax.shard_map(
        local,
        mesh=mesh,
        in_specs=placed,
        out_specs=(
            P("tp", None),
            P("tp", None),
            P("worker", "tp", None),
            P("worker", "tp", None),
            P("worker", None),
            P("worker", "tp", None),
            P("worker", "tp", None),
            P("worker", "tp", None),
        ),
        check_vma=False,
    )
```

```python
import jax
import jax.numpy as jnp
from jax import lax
from jax.sharding import PartitionSpec as P

OUTER_RATE = 0.7
OUTER_MOMENTUM = 0.9
NORM_EPS = 1e-06

SIDE_Z, SIDE_Y, SIDE_X = 2, 4, 4


def gelu_tanh(values):
    return jax.nn.gelu(values, approximate=True)


def gelu_grad(pre_act, upstream):
    outputs = jax.vjp(gelu_tanh, pre_act)
    return outputs[1](upstream)[0]


def place(z, y, x):
    return (z % SIDE_Z) * SIDE_Y * SIDE_X + (y % SIDE_Y) * SIDE_X + x % SIDE_X


def shift(block, axis, by):
    step = {"z": 0, "y": 0, "x": 0}
    step[axis] = by
    pairs = [
        (place(z, y, x), place(z + step["z"], y + step["y"], x + step["x"]))
        for z in range(SIDE_Z)
        for y in range(SIDE_Y)
        for x in range(SIDE_X)
    ]
    return lax.ppermute(block, "tp", pairs)


def after(value, *others):
    return lax.optimization_barrier((value, others))[0]


def plane_groups():
    return [
        [place(z, y, x) for y in range(SIDE_Y) for x in range(SIDE_X)] for z in range(SIDE_Z)
    ]


def gather(rows):
    half = rows.shape[0] // 2
    other = shift(rows, "z", 1)
    block = jnp.concatenate([rows[:half], other[:half], rows[half:], other[half:]], axis=0)
    return lax.all_gather(block, "tp", axis=0, tiled=True, axis_index_groups=plane_groups())


def turn(blocks, axis, start):
    both = jnp.concatenate([blocks, blocks], axis=axis)
    return lax.dynamic_slice_in_dim(both, lax.rem(start, 4), 4, axis)


def turned_halves(rows):
    me = lax.axis_index("tp")
    my_y, my_x = lax.rem(lax.div(me, SIDE_X), SIDE_Y), lax.rem(me, SIDE_X)
    width = rows.shape[1]
    blocks = rows.reshape(SIDE_Y, SIDE_X, -1, width)
    half = blocks.shape[2] // 2
    first = turn(turn(blocks[:, :, :half], 0, my_y + 1), 1, my_x)
    second = turn(turn(blocks[:, :, half:].transpose(1, 0, 2, 3), 0, my_x + 1), 1, my_y)
    return first.reshape(-1, width), second.reshape(-1, width)


def line_sum(row, axis):
    return row + shift(row, axis, 1) + shift(row, axis, -1) + shift(row, axis, 2)


def total(*terms):
    result = terms[0].astype(jnp.float32)
    for term in terms[1:]:
        result = result + term.astype(jnp.float32)
    return result.astype(jnp.bfloat16)


def eighths(rows):
    size = rows.shape[0] // 8
    cuts = (0, 1, 3, 5, 6, 7, 8)
    return [rows[a * size : b * size] for a, b in zip(cuts, cuts[1:])]


def scatter_first_shares(halves, weights):
    return [
        jnp.dot(part, weights, preferred_element_type=jnp.float32).astype(jnp.bfloat16)
        for rows in halves
        for part in eighths(rows)[1:3]
    ]


def scatter_far(shares):
    return tuple(
        shift(part, axis, by) for part, axis, by in zip(shares, ("y", "y", "x", "x"), (1, -1, 1, -1))
    )


def scatter_next(halves, weights, got):
    ends = ()
    for rows, axis, (up, down) in zip(halves, ("y", "x"), (got[:2], got[2:])):
        parts = eighths(rows)
        size = parts[0].shape[0]
        ahead = jnp.dot(parts[0], weights, preferred_element_type=jnp.float32)
        behind = jnp.dot(parts[3], weights, preferred_element_type=jnp.float32)
        ends += (shift(total(ahead, up[size:]), axis, 1), shift(total(behind, down[:size]), axis, -1))
    return ends


def scatter_end(halves, weights, got, ends):
    lines = ()
    for rows, (up, down), (last_up, last_down) in zip(halves, (got[:2], got[2:]), (ends[:2], ends[2:])):
        parts = eighths(rows)
        size = parts[0].shape[0]
        low = jnp.dot(parts[4], weights, preferred_element_type=jnp.float32)
        high = jnp.dot(parts[5], weights, preferred_element_type=jnp.float32)
        lines += (total(low, last_up, down[size:]), total(high, up[:size], last_down))
    return lines


def scatter_near(lines):
    own, other = [], []
    for (low, high), axis in zip((lines[:2], lines[2:]), ("x", "y")):
        half = low.shape[0] // 2
        sums = total(
            low[:half], shift(low[half:], axis, 1), shift(high[half:], axis, -1), shift(high[:half], axis, 2)
        )
        own.append(sums[: half // 2])
        other.append(sums[half // 2 :])
    return jnp.concatenate(own, axis=0), jnp.concatenate(other, axis=0)


def dot(left, right, contract, dtype=jnp.float32):
    return lax.dot_general(
        left, right, ((contract[0], contract[1]), ((), ())), preferred_element_type=jnp.float32
    ).astype(dtype)


def local(
    global_params, momentum, local_params, inputs, out_grad, token_ids, gain, w_gate, w_up, w_down
):
    delta = global_params - local_params[0]
    workers = lax.axis_size("worker")
    delta_sum = lax.psum(delta.astype(jnp.bfloat16), "worker")
    gain_row = gain[0]
    gate_w = w_gate[0]
    up_w = w_up[0]
    down_w = w_down[0]
    tokens_f = inputs[0].astype(jnp.float32)
    inv_rms = lax.rsqrt(jnp.mean(tokens_f * tokens_f, axis=1, keepdims=True) + NORM_EPS)
    scaled = tokens_f * inv_rms
    normed = (scaled * gain_row[None, :]).astype(jnp.bfloat16)
    barrier = lax.optimization_barrier
    masked = jnp.where((token_ids[0] != 0)[:, None], out_grad[0], jnp.zeros_like(out_grad[0]))
    last, first = ((1,), (1,)), ((0,), (0,))
    plain = ((1,), (0,))
    normed_all = gather(normed)
    masked_all = gather(masked)

    def forward(rows):
        gate_pre = dot(rows, gate_w, last)
        up_pre = dot(rows, up_w, last)
        return gate_pre, up_pre, (gelu_tanh(gate_pre) * up_pre).astype(jnp.bfloat16)

    def backward(rows, gate_pre, up_pre):
        hid_grad = dot(rows, down_w, last)
        gate_grad = gelu_grad(gate_pre, hid_grad * up_pre).astype(jnp.bfloat16)
        up_grad = (hid_grad * gelu_tanh(gate_pre)).astype(jnp.bfloat16)
        return jnp.concatenate([gate_grad, up_grad], axis=1)

    both_w = jnp.concatenate([gate_w, up_w], axis=0)
    gate_pre, up_pre, hidden = forward(normed_all)
    halves = turned_halves(hidden)
    ffn_far = scatter_far(scatter_first_shares(halves, down_w))
    ffn_ends = scatter_next(halves, down_w, ffn_far)
    ffn_lines = scatter_end(halves, down_w, ffn_far, ffn_ends)
    ffn_own, ffn_back = scatter_near(ffn_lines)
    masked_all, ffn_back, delta_sum = barrier((masked_all, ffn_back, delta_sum))
    both = backward(masked_all, gate_pre, up_pre)
    halves = turned_halves(both)
    shares, both, masked_all = barrier((scatter_first_shares(halves, both_w), both, masked_all))
    grad_far = scatter_far(shares)
    both_done = dot(both, normed_all, first, jnp.bfloat16)
    units = gate_w.shape[0]
    grad_gate, grad_up = both_done[:units], both_done[units:]
    gain_share = jnp.sum(both_done.astype(jnp.float32) * both_w.astype(jnp.float32), axis=0)[None]
    gain_share, grad_far = barrier((gain_share, grad_far))
    grad_ends = scatter_next(halves, both_w, grad_far)
    gain_share, grad_ends = barrier((line_sum(gain_share, "x"), grad_ends))
    grad_lines = scatter_end(halves, both_w, grad_far, grad_ends)
    grad_own, grad_back = scatter_near(grad_lines)
    ffn_sum = total(ffn_own, shift(ffn_back, "z", 1))
    grad_down = dot(hidden, masked_all, first, jnp.bfloat16)
    average = delta_sum.astype(jnp.float32) / workers
    new_momentum = OUTER_MOMENTUM * momentum + average
    new_params = global_params - OUTER_RATE * (average + OUTER_MOMENTUM * new_momentum)
    gain_share, grad_back, ffn_sum, grad_down = barrier(
        (line_sum(gain_share, "y"), grad_back, ffn_sum, grad_down)
    )
    grad_other = shift(grad_back, "z", 1)
    grad_gain = (gain_share + shift(gain_share, "z", 1))[0] / gain_row
    normed_grad = grad_own.astype(jnp.float32) + grad_other.astype(jnp.float32)
    weighted = normed_grad * gain_row[None, :]
    centred = weighted - scaled * jnp.mean(weighted * scaled, axis=1, keepdims=True)
    grad_input = (inv_rms * centred).astype(jnp.bfloat16)
    return (
        new_params,
        new_momentum,
        ffn_sum[None],
        grad_input[None],
        grad_gain[None],
        grad_gate[None],
        grad_up[None],
        grad_down[None],
    )


def solution(mesh):
    placed = (
        P("tp", None),
        P("tp", None),
        P("worker", "tp", None),
        P("worker", "tp", None),
        P("worker", "tp", None),
        P("worker", "tp"),
        P("worker", None),
        P("worker", "tp", None),
        P("worker", "tp", None),
        P("worker", "tp", None),
    )
    return jax.shard_map(
        local,
        mesh=mesh,
        in_specs=placed,
        out_specs=(
            P("tp", None),
            P("tp", None),
            P("worker", "tp", None),
            P("worker", "tp", None),
            P("worker", None),
            P("worker", "tp", None),
            P("worker", "tp", None),
            P("worker", "tp", None),
        ),
        check_vma=False,
    )
```

```python
import jax
import jax.numpy as jnp
from jax import lax
from jax.sharding import PartitionSpec as P

OUTER_RATE = 0.7
OUTER_MOMENTUM = 0.9
NORM_EPS = 1e-06

SIDE_Z, SIDE_Y, SIDE_X = 2, 4, 4


def gelu_tanh(values):
    return jax.nn.gelu(values, approximate=True)


def gelu_grad(pre_act, upstream):
    outputs = jax.vjp(gelu_tanh, pre_act)
    return outputs[1](upstream)[0]


def place(z, y, x):
    return (z % SIDE_Z) * SIDE_Y * SIDE_X + (y % SIDE_Y) * SIDE_X + x % SIDE_X


def shift(block, axis, by):
    step = {"z": 0, "y": 0, "x": 0}
    step[axis] = by
    pairs = [
        (place(z, y, x), place(z + step["z"], y + step["y"], x + step["x"]))
        for z in range(SIDE_Z)
        for y in range(SIDE_Y)
        for x in range(SIDE_X)
    ]
    return lax.ppermute(block, "tp", pairs)


def after(value, *others):
    return lax.optimization_barrier((value, others))[0]


def plane_groups():
    return [
        [place(z, y, x) for y in range(SIDE_Y) for x in range(SIDE_X)] for z in range(SIDE_Z)
    ]


def gather(rows):
    half = rows.shape[0] // 2
    other = shift(rows, "z", 1)
    block = jnp.concatenate([rows[:half], other[:half], rows[half:], other[half:]], axis=0)
    return lax.all_gather(block, "tp", axis=0, tiled=True, axis_index_groups=plane_groups())


def turn(blocks, axis, start):
    both = jnp.concatenate([blocks, blocks], axis=axis)
    return lax.dynamic_slice_in_dim(both, lax.rem(start, 4), 4, axis)


def turned_halves(rows):
    me = lax.axis_index("tp")
    my_y, my_x = lax.rem(lax.div(me, SIDE_X), SIDE_Y), lax.rem(me, SIDE_X)
    width = rows.shape[1]
    blocks = rows.reshape(SIDE_Y, SIDE_X, -1, width)
    half = blocks.shape[2] // 2
    first = turn(turn(blocks[:, :, :half], 0, my_y + 1), 1, my_x)
    second = turn(turn(blocks[:, :, half:].transpose(1, 0, 2, 3), 0, my_x + 1), 1, my_y)
    return first.reshape(-1, width), second.reshape(-1, width)


def line_sum(row, axis):
    return row + shift(row, axis, 1) + shift(row, axis, -1) + shift(row, axis, 2)


def total(*terms):
    result = terms[0].astype(jnp.float32)
    for term in terms[1:]:
        result = result + term.astype(jnp.float32)
    return result.astype(jnp.bfloat16)


def eighths(rows):
    size = rows.shape[0] // 8
    cuts = (0, 1, 3, 5, 6, 7, 8)
    return [rows[a * size : b * size] for a, b in zip(cuts, cuts[1:])]


def scatter_first_shares(halves, weights):
    return [
        jnp.dot(part, weights, preferred_element_type=jnp.float32).astype(jnp.bfloat16)
        for rows in halves
        for part in eighths(rows)[1:3]
    ]


def scatter_far(shares):
    return tuple(
        shift(part, axis, by) for part, axis, by in zip(shares, ("y", "y", "x", "x"), (1, -1, 1, -1))
    )


def scatter_next(halves, weights, got):
    ends = ()
    for rows, axis, (up, down) in zip(halves, ("y", "x"), (got[:2], got[2:])):
        parts = eighths(rows)
        size = parts[0].shape[0]
        ahead = jnp.dot(parts[0], weights, preferred_element_type=jnp.float32)
        behind = jnp.dot(parts[3], weights, preferred_element_type=jnp.float32)
        ends += (shift(total(ahead, up[size:]), axis, 1), shift(total(behind, down[:size]), axis, -1))
    return ends


def scatter_end(halves, weights, got, ends):
    lines = ()
    for rows, (up, down), (last_up, last_down) in zip(halves, (got[:2], got[2:]), (ends[:2], ends[2:])):
        parts = eighths(rows)
        size = parts[0].shape[0]
        low = jnp.dot(parts[4], weights, preferred_element_type=jnp.float32)
        high = jnp.dot(parts[5], weights, preferred_element_type=jnp.float32)
        lines += (total(low, last_up, down[size:]), total(high, up[:size], last_down))
    return lines


def scatter_near(lines):
    own, other = [], []
    for (low, high), axis in zip((lines[:2], lines[2:]), ("x", "y")):
        half = low.shape[0] // 2
        sums = total(
            low[:half], shift(low[half:], axis, 1), shift(high[half:], axis, -1), shift(high[:half], axis, 2)
        )
        own.append(sums[: half // 2])
        other.append(sums[half // 2 :])
    return jnp.concatenate(own, axis=0), jnp.concatenate(other, axis=0)


def dot(left, right, contract, dtype=jnp.float32):
    return lax.dot_general(
        left, right, ((contract[0], contract[1]), ((), ())), preferred_element_type=jnp.float32
    ).astype(dtype)


def local(
    global_params, momentum, local_params, inputs, out_grad, token_ids, gain, w_gate, w_up, w_down
):
    delta = global_params - local_params[0]
    workers = lax.axis_size("worker")
    delta_sum = lax.psum(delta.astype(jnp.bfloat16), "worker")
    gain_row = gain[0]
    gate_w = w_gate[0]
    up_w = w_up[0]
    down_w = w_down[0]
    tokens_f = inputs[0].astype(jnp.float32)
    inv_rms = lax.rsqrt(jnp.mean(tokens_f * tokens_f, axis=1, keepdims=True) + NORM_EPS)
    scaled = tokens_f * inv_rms
    normed = (scaled * gain_row[None, :]).astype(jnp.bfloat16)
    barrier = lax.optimization_barrier
    masked = jnp.where((token_ids[0] != 0)[:, None], out_grad[0], jnp.zeros_like(out_grad[0]))
    last, first = ((1,), (1,)), ((0,), (0,))
    plain = ((1,), (0,))
    normed_all = gather(normed)
    masked_all = gather(masked)

    def forward(rows):
        gate_pre = dot(rows, gate_w, last)
        up_pre = dot(rows, up_w, last)
        return gate_pre, up_pre, (gelu_tanh(gate_pre) * up_pre).astype(jnp.bfloat16)

    def backward(rows, gate_factor, up_factor):
        hid_grad = dot(rows, down_w, last)
        gate_grad = (hid_grad * gate_factor).astype(jnp.bfloat16)
        up_grad = (hid_grad * up_factor).astype(jnp.bfloat16)
        return jnp.concatenate([gate_grad, up_grad], axis=1)

    both_w = jnp.concatenate([gate_w, up_w], axis=0)
    gate_pre, up_pre, hidden = forward(normed_all)
    halves = turned_halves(hidden)
    ffn_far = scatter_far(scatter_first_shares(halves, down_w))
    ffn_ends = scatter_next(halves, down_w, ffn_far)
    ffn_lines = scatter_end(halves, down_w, ffn_far, ffn_ends)
    ffn_own, ffn_back = scatter_near(ffn_lines)
    factors = (gelu_grad(gate_pre, up_pre), gelu_tanh(gate_pre))
    masked_all, ffn_back, delta_sum, factors = barrier((masked_all, ffn_back, delta_sum, factors))
    both = backward(masked_all, *factors)
    halves = turned_halves(both)
    shares, both, masked_all = barrier((scatter_first_shares(halves, both_w), both, masked_all))
    grad_far = scatter_far(shares)
    both_done = dot(both, normed_all, first, jnp.bfloat16)
    units = gate_w.shape[0]
    grad_gate, grad_up = both_done[:units], both_done[units:]
    gain_share = jnp.sum(both_done.astype(jnp.float32) * both_w.astype(jnp.float32), axis=0)[None]
    gain_share, grad_far, ffn_back = barrier((gain_share, grad_far, ffn_back))
    grad_ends = scatter_next(halves, both_w, grad_far)
    gain_share, grad_ends = barrier((line_sum(gain_share, "x"), grad_ends))
    grad_lines = scatter_end(halves, both_w, grad_far, grad_ends)
    grad_own, grad_back = scatter_near(grad_lines)
    ffn_sum = total(ffn_own, shift(ffn_back, "z", 1))
    grad_down = dot(hidden, masked_all, first, jnp.bfloat16)
    average = delta_sum.astype(jnp.float32) / workers
    new_momentum = OUTER_MOMENTUM * momentum + average
    new_params = global_params - OUTER_RATE * (average + OUTER_MOMENTUM * new_momentum)
    gain_share, grad_back, ffn_sum, grad_down = barrier(
        (line_sum(gain_share, "y"), grad_back, ffn_sum, grad_down)
    )
    grad_other = shift(grad_back, "z", 1)
    grad_gain = (gain_share + shift(gain_share, "z", 1))[0] / gain_row
    normed_grad = grad_own.astype(jnp.float32) + grad_other.astype(jnp.float32)
    weighted = normed_grad * gain_row[None, :]
    centred = weighted - scaled * jnp.mean(weighted * scaled, axis=1, keepdims=True)
    grad_input = (inv_rms * centred).astype(jnp.bfloat16)
    return (
        new_params,
        new_momentum,
        ffn_sum[None],
        grad_input[None],
        grad_gain[None],
        grad_gate[None],
        grad_up[None],
        grad_down[None],
    )


def solution(mesh):
    placed = (
        P("tp", None),
        P("tp", None),
        P("worker", "tp", None),
        P("worker", "tp", None),
        P("worker", "tp", None),
        P("worker", "tp"),
        P("worker", None),
        P("worker", "tp", None),
        P("worker", "tp", None),
        P("worker", "tp", None),
    )
    return jax.shard_map(
        local,
        mesh=mesh,
        in_specs=placed,
        out_specs=(
            P("tp", None),
            P("tp", None),
            P("worker", "tp", None),
            P("worker", "tp", None),
            P("worker", None),
            P("worker", "tp", None),
            P("worker", "tp", None),
            P("worker", "tp", None),
        ),
        check_vma=False,
    )
```
